32 devices in a mesh: trk: 8 (over z, x), cam: 4 (over y, core).
Axes of the slice: x: 2, y: 2, z: 4, core: 2. Of those that a mesh axis runs over, the one named last changes fastest.
Arguments:
- residuals: float32 [2, 24576], P(None, ('trk', 'cam')), may hold values from -6 to 6
- camera_jac: float32 [18, 24576], P(None, ('trk', 'cam')), may hold values from -9 to 9
- point_jac: float32 [6, 24576], P(None, ('trk', 'cam')), may hold values from -6 to 6
- obs_index: int32 [3, 24576], P(None, ('trk', 'cam')), may hold values from 0 to 767, as said below
- damping: float32 [2048], P('trk'), may hold values from 0.5 to 4
Outputs:
- elimination_tiles: float32 [8, 4, 7, 20736], P('trk', 'cam')
The draws below stay inside these ranges and needn't reach their ends.
Inputs may be any that keep to these rules, and one draw needn't show every extreme that they name: For each c and e, the values obs_index[0, n] of the rows n = ((t * 4 + c) * 8 + e) * 96 + q over all t and q are a permutation of 0 to 767. The camera obs_index[1, n] of such a row lies in a block (camera // 16) among 2 * e to 2 * e + 7, taken modulo 16. obs_index[2, n] is 1 for a live observation and 0 for a padded slot.
All inputs are finite; a program needn't handle non-finite values.
Results may differ from the reference program's by a relative error of at most 0.0003.
Values sent between devices are 32-bit elements; how exact they have to be, the bound alone decides.
A program may use at most 64 MiB of HBM per device.

```python
import math
import jax
import jax.numpy as jnp
from jax import lax

CAMERAS_PER_BLK = 16
TS = 144
HOPS = 3
WIN = 8
TILE_OWN = 7
SLOTS = 12
KC = 3
TRK_DEV = 256
SPR = 96
TRACKS = 2048
ROWS = 24576
CAMERA_BLOCKS = 16
N_TRK = 8
N_CAM = 4


def draw_obs_index(key, part):
    key_shuffle = jax.random.fold_in(key, 11)
    key_block = jax.random.fold_in(key, 12)
    camera_key_value = jax.random.fold_in(key, 13)
    key_alive = jax.random.fold_in(key, 14)
    row_keys = jax.random.split(key_shuffle, N_CAM * N_TRK)

    def shuffle(single_key):
        return jax.random.permutation(single_key, TRK_DEV * KC)
    shuffled = jax.vmap(shuffle)(row_keys).reshape((N_CAM, N_TRK, N_TRK, SPR))
    position = jnp.transpose(shuffled, (2, 0, 1, 3)).astype(jnp.int32)
    launch_layout = (N_TRK, N_CAM, N_TRK, SPR)
    offset = jax.random.randint(key_block, launch_layout, 0, WIN)
    offset = offset.at[0, 0, N_TRK - 1, 0].set(1)
    target = 2 * jnp.arange(N_TRK, dtype=jnp.int32)[None, None, :, None]
    block_number = jnp.mod(target + offset, CAMERA_BLOCKS)
    within = jax.random.randint(camera_key_value, launch_layout, 0, CAMERAS_PER_BLK)
    within = within.at[0, 0, N_TRK - 1, 0].set(CAMERAS_PER_BLK - 1)
    camera_view = block_number * CAMERAS_PER_BLK + within
    alive_mask = (jax.random.randint(key_alive, launch_layout, 0, 4) > 0).astype(jnp.int32)
    return jnp.stack([position, camera_view.astype(jnp.int32), alive_mask]).reshape((3, -1)).astype(jnp.int32)


def shard_levels(own_key, shape, pieces, low, top_value):
    def one(dim, blocks):
        draws = jax.random.uniform(jax.random.fold_in(jax.random.fold_in(own_key, 6), dim), (blocks,), jnp.float32, low / len(pieces), top_value / len(pieces))
        return jnp.repeat(jnp.exp(draws), shape[dim] // blocks).reshape((-1,) + (1,) * (len(shape) - dim - 1))

    gain = one(*pieces[0])
    for cut in pieces[1:]:
        gain = gain * one(*cut)
    return gain


def bell_draw(key, dims, scale, bound, pieces=(), held_as=jnp.bfloat16):
    drawn = scale * jax.random.normal(key, dims, jnp.float32)
    if pieces:
        drawn = drawn * shard_levels(key, dims, pieces, -0.22, 0.18)
    return jnp.clip(drawn, -bound, bound).astype(held_as)


def setup_inputs(seed: int = 0) -> dict:
    keys = jax.random.split(jax.random.key(seed), 6)
    return {
        "residuals": bell_draw(keys[0], (2, ROWS), 1.0, 6.0, ((1, 32),), jnp.float32),
        "camera_jac": bell_draw(keys[1], (18, ROWS), 1.5, 9.0, ((1, 32),), jnp.float32),
        "point_jac": bell_draw(keys[2], (6, ROWS), 1.0, 6.0, ((1, 32),), jnp.float32),
        "obs_index": draw_obs_index(jax.random.fold_in(keys[5], 71), 0),
        "damping": jnp.clip(jnp.exp(math.log(4.0) - 2.0794415 * jax.random.uniform(keys[4], (TRACKS,), jnp.float32) ** shard_levels(keys[4], (TRACKS,), ((0, 8),), -0.2, 0.2)), 0.5, 4.0),
    }


HUBER_DELTA = 1.0
UPPER_PAIRS = ((0, 0), (0, 1), (0, 2), (1, 1), (1, 2), (2, 2))
DIAGONAL_MASK = (1.0, 0.0, 0.0, 1.0, 0.0, 1.0)

def huber_weights(residuals, alive_mask):
    magnitude = jnp.sqrt(residuals[0] * residuals[0] + residuals[1] * residuals[1])
    return alive_mask.astype(jnp.float32) * (HUBER_DELTA / jnp.maximum(magnitude, HUBER_DELTA))

def coupling(camera_jac, point_jac, weights):
    first = camera_jac[:9, None] * point_jac[None, :3]
    second = camera_jac[9:, None] * point_jac[None, 3:]
    joined = (first + second) * weights
    return joined.reshape((27,) + weights.shape)

def point_terms(point_jac, weights):
    return jnp.stack([weights * (point_jac[k] * point_jac[l] + point_jac[3 + k] * point_jac[3 + l]) for k, l in UPPER_PAIRS])

def point_inverse(points, damping):
    diagonal = jnp.asarray(DIAGONAL_MASK, dtype=jnp.float32)[:, None]
    full_block = points + diagonal * damping[None]
    a, b, c, d, e, f = (full_block[0], full_block[1], full_block[2], full_block[3], full_block[4], full_block[5])
    cofactor = jnp.stack([d * f - e * e, c * e - b * f, b * e - c * d, a * f - c * c, b * c - a * e, a * d - b * b])
    determinant = a * cofactor[0] + b * cofactor[1] + c * cofactor[2]
    scaled = cofactor / determinant
    entry_order = (0, 1, 2, 1, 3, 4, 2, 4, 5)
    return jnp.stack([scaled[i] for i in entry_order]).reshape((3, 3) + damping.shape)

def block_panels(couplings, visible_block, camera_position, offsets):
    block_match = (visible_block[None] == offsets[:, None, None]).astype(jnp.float32)
    position_equal = (camera_position[None] == jnp.arange(CAMERAS_PER_BLK, dtype=jnp.int32)[:, None, None]).astype(jnp.float32)
    selector = block_match[:, None] * position_equal[None]
    panels = jnp.einsum('misp,xsp->mixp', selector, couplings, precision=lax.Precision.HIGHEST)
    return panels.reshape((offsets.shape[0], TS, 3, couplings.shape[-1]))

def solve_panels(panels, inverse):
    return jnp.einsum('makp,klp->malp', panels, inverse, precision=lax.Precision.HIGHEST)

def tile_products(left_flat, right_flat):
    return lax.dot_general(left_flat, right_flat, (((1,), (1,)), ((), ())), precision=lax.Precision.HIGHEST)

def reference(residuals, camera_jac, point_jac, obs_index, damping):
    columns = jnp.arange(N_CAM, dtype=jnp.int32)[:, None] * (KC * TRK_DEV)
    offsets = jnp.arange(WIN, dtype=jnp.int32)
    row_block = offsets[:, None] + 0 * offsets[None, :]
    col_block = offsets[None, :] + 0 * offsets[:, None]
    owner_step = row_block // 2
    column_index = 2 * (row_block % 2) + col_block % 2
    slot_index = col_block // 2 - row_block // 2 + HOPS

    def pick(array, tile_strip):
        shaped = array.reshape((array.shape[0], N_TRK, N_CAM, N_TRK, SPR))
        taken = lax.dynamic_index_in_dim(shaped, tile_strip, 3, keepdims=False)
        return jnp.transpose(taken, (0, 2, 1, 3)).reshape((array.shape[0], N_CAM * N_TRK * SPR))

    def place(values, target):
        placed = jnp.zeros((values.shape[0], SLOTS * TRK_DEV), values.dtype).at[:, target].set(values)
        return placed.reshape((values.shape[0], SLOTS, TRK_DEV))

    def add_slab(summed, tile_strip):
        indices = pick(obs_index, tile_strip)
        target = (columns + indices[0].reshape((N_CAM, N_TRK * SPR))).reshape(-1)
        residual_slots = place(pick(residuals, tile_strip), target)
        camera_slots = place(pick(camera_jac, tile_strip), target)
        point_slots = place(pick(point_jac, tile_strip), target)
        index_positions = place(indices[1:], target)
        weights = huber_weights(residual_slots, index_positions[1])
        couplings = coupling(camera_slots, point_slots, weights)
        points = point_terms(point_slots, weights).sum(axis=1)
        slab_damping = lax.dynamic_slice_in_dim(damping, tile_strip * TRK_DEV, TRK_DEV)
        inverse = point_inverse(points, slab_damping)
        visible_block = jnp.mod(index_positions[0] // CAMERAS_PER_BLK - 2 * tile_strip, CAMERA_BLOCKS)
        camera_position = index_positions[0] % CAMERAS_PER_BLK
        panels = block_panels(couplings, visible_block, camera_position, offsets)
        left_panels = solve_panels(panels, inverse)
        product = tile_products(left_panels.reshape((WIN * TS, -1)), panels.reshape((WIN * TS, -1)))
        tiles = product.reshape((WIN, TS, WIN, TS)).transpose((0, 2, 1, 3)).reshape((WIN, WIN, TS * TS))
        owner = jnp.mod(tile_strip + owner_step, N_TRK)
        return (summed.at[owner, column_index, slot_index].add(tiles), None)
    initial = jnp.zeros((N_TRK, N_CAM, TILE_OWN, TS * TS), jnp.float32)
    summed, _ = lax.scan(add_slab, initial, jnp.arange(N_TRK, dtype=jnp.int32))
    return summed
```

```python
import functools

import jax
import jax.numpy as jnp
import numpy as np
from jax import lax
from jax.experimental import pallas as pl
from jax.experimental.pallas import tpu as pltpu
from jax.sharding import PartitionSpec as P

CAMERAS_PER_BLK = 16
TS = 144
HOPS = 3
OWNERS = HOPS + 1
TILES = 2 * HOPS + 1
KC = 3
TRACKS = 256
SLOTS = 12
LANES = 128
MSG = 152
DIRECT_DEVICES = 8
MESH = pl.DeviceIdType.MESH


def split(x):
    high = x.astype(jnp.bfloat16)
    low = (x - high.astype(jnp.float32)).astype(jnp.bfloat16)
    return high, low


def scaled_rows(residuals, camera_jac, point_jac, index):
    first, second = residuals[0:1], residuals[1:2]
    magnitude = jnp.sqrt(first * first + second * second)
    weight = index[2:3].astype(jnp.float32) / jnp.maximum(magnitude, 1.0)
    root = jnp.sqrt(weight)
    return (
        camera_jac * root,
        point_jac * root,
        index[1:2].astype(jnp.float32),
        index[0:1].astype(jnp.float32),
    )


def exchange_body(direct, n, *refs):
    if direct:
        res_ref, cam_ref, pnt_ref, idx_ref, damp_ref, got_ref = refs[:6]
        rows_ref, send_ref, recv_ref, ssem1, rsem1, ssem2, rsem2, ssem3, rsem3 = refs[6:]
    else:
        rows_ref, damp_ref, got_ref = refs[:3]
        ssem2, rsem2, ssem3, rsem3 = refs[3:]
    me = lax.axis_index("trk")
    col = lax.axis_index("cam")
    core = col + 1 - 2 * lax.rem(col, 2)
    side = lax.rem(col + 2, 4)

    def ahead(by):
        return lax.rem(me + by, n)

    barrier = pltpu.get_barrier_semaphore()
    steps = range(1, n) if direct else (1, 2, 3, n - 3, n - 2, n - 1)
    for by in steps:
        pl.semaphore_signal(barrier, inc=1, device_id=(ahead(by), col), device_id_type=MESH)
    for other in (core, side):
        pl.semaphore_signal(barrier, inc=1, device_id=(me, other), device_id_type=MESH)

    if direct:
        width = rows_ref.shape[1] // n
        cj, pj, camera, position = scaled_rows(res_ref[...], cam_ref[...], pnt_ref[...], idx_ref[...])
        rows_ref[0:18] = cj
        rows_ref[18:24] = pj
        rows_ref[24:25] = camera
        rows_ref[25:26] = position
        rows_ref[26:32] = jnp.zeros((6, rows_ref.shape[1]), jnp.float32)
        rows = rows_ref[...]
        lane = lax.broadcasted_iota(jnp.int32, (32, LANES), 1)
        row = lax.broadcasted_iota(jnp.int32, (32, LANES), 0)
        fill = jnp.where(row == 25, -1.0, 0.0)
        for e in range(n):
            start = e * width
            piece = rows if start == 0 else pltpu.roll(rows, rows.shape[1] - start, 1)
            send_ref[e] = jnp.where(lane < width, piece[:, :LANES], fill)
    pl.semaphore_wait(barrier, len(steps) + 2)

    if direct:
        copies = []
        for by in range(1, n):
            copy = pltpu.make_async_remote_copy(
                src_ref=send_ref.at[ahead(by)],
                dst_ref=recv_ref.at[by],
                send_sem=ssem1.at[by],
                recv_sem=rsem1.at[by],
                device_id=(ahead(by), col),
                device_id_type=MESH,
            )
            copy.start()
            copies.append(copy)
        recv_ref[0] = send_ref[me]
        for copy in copies:
            copy.wait()
        chunks = [recv_ref[k] for k in range(n)]
    else:
        chunks = [rows_ref[:, k * LANES : (k + 1) * LANES] for k in range(rows_ref.shape[1] // LANES)]

    slot = lax.broadcasted_iota(jnp.int32, (KC * TRACKS, LANES), 0).astype(jnp.float32)
    places, values = [], []
    for chunk in chunks:
        places.append(jnp.where(slot == chunk[25:26], 1.0, 0.0).astype(jnp.bfloat16))
        high, low = split(chunk)
        values.append(jnp.concatenate([high, low], axis=0))
    placed = lax.dot_general(
        jnp.concatenate(values, axis=1),
        jnp.concatenate(places, axis=1),
        (((1,), (1,)), ((), ())),
        preferred_element_type=jnp.float32,
    )
    placed = placed[:32] + placed[32:]
    tiles = KC * TRACKS // LANES
    for r in range(3):
        for l in range(tiles):
            at = (r * tiles + l) * 8
            got_ref[0, 0, at : at + 8] = placed[8 * r : 8 * r + 8, l * LANES : (l + 1) * LANES]
    for l in range(tiles):
        got_ref[0, 0, 144 + l : 145 + l] = placed[24:25, l * LANES : (l + 1) * LANES]
    for l in range(2):
        got_ref[0, 0, 150 + l : 151 + l] = damp_ref[:, l * LANES : (l + 1) * LANES]

    def send(src, dst, ssem, rsem, device):
        copy = pltpu.make_async_remote_copy(
            src_ref=src, dst_ref=dst, send_sem=ssem, recv_sem=rsem, device_id=device, device_id_type=MESH
        )
        copy.start()
        return copy

    along = [None]
    for h in range(1, OWNERS):
        along.append(
            send(got_ref.at[0, 0], got_ref.at[h, 0], ssem2.at[h], rsem2.at[h], (ahead(h), col))
        )
    sides, cores, passed = [], [], []
    for h in range(OWNERS):
        if h:
            along[h].wait_recv()
        sides.append(
            send(got_ref.at[h, 0], got_ref.at[h, 2], ssem3.at[h, 2], rsem3.at[h, 2], (me, side))
        )
        cores.append(
            send(got_ref.at[h, 0], got_ref.at[h, 1], ssem3.at[h, 1], rsem3.at[h, 1], (me, core))
        )
    for h in range(OWNERS):
        sides[h].wait_recv()
        passed.append(
            send(got_ref.at[h, 2], got_ref.at[h, 3], ssem3.at[h, 3], rsem3.at[h, 3], (me, core))
        )
    for h in range(OWNERS):
        cores[h].wait_recv()
        passed[h].wait_recv()
    for copy in along[1:] + sides + cores + passed:
        copy.wait_send()


def exchange(n, direct, damping, *arrays):
    vmem = pl.BlockSpec(memory_space=pltpu.VMEM)
    dma = pltpu.SemaphoreType.DMA
    scratch = []
    if direct:
        scratch += [
            pltpu.VMEM((32, arrays[0].shape[1]), jnp.float32),
            pltpu.VMEM((n, 32, LANES), jnp.float32),
            pltpu.VMEM((n, 32, LANES), jnp.float32),
            dma((n,)),
            dma((n,)),
        ]
    scratch += [dma((OWNERS,)), dma((OWNERS,)), dma((OWNERS, 4)), dma((OWNERS, 4))]
    return pl.pallas_call(
        functools.partial(exchange_body, direct, n),
        out_shape=jax.ShapeDtypeStruct((OWNERS, 4, MSG, LANES), jnp.float32),
        in_specs=[vmem] * (len(arrays) + 1),
        out_specs=vmem,
        scratch_shapes=scratch,
        compiler_params=pltpu.CompilerParams(
            collective_id=0, has_side_effects=True, vmem_limit_bytes=32 * 2**20
        ),
        name="exchange",
    )(*arrays, damping.reshape(1, TRACKS))


def tiles_body(n, got_ref, repeat_ref, group_ref, out_ref, rep, coup, view, left, right, acc_a, acc_b):
    me = lax.axis_index("trk")
    col = lax.axis_index("cam")
    cameras = 2 * n * CAMERAS_PER_BLK
    left_parity = col // 2
    right_parity = lax.rem(col, 2)
    acc_a[...] = jnp.zeros_like(acc_a)
    acc_b[...] = jnp.zeros_like(acc_b)

    def jac_tile(h, part, r, l):
        return got_ref[h, part, (r * 6 + l) * 8 : (r * 6 + l) * 8 + 8]

    def per_slab(h, _):
        slab = lax.rem(me + n - h, n)

        def per_part(part, sums):
            sums = list(sums)
            blocks = [
                jnp.concatenate([jac_tile(h, part, r, l) for r in range(3)], axis=0) for l in range(6)
            ]
            values = jnp.concatenate(blocks, axis=1)
            high, low = split(values)
            rep[...] = lax.dot_general(
                repeat_ref[...],
                jnp.concatenate([high, low], axis=0),
                (((1,), (0,)), ((), ())),
                preferred_element_type=jnp.float32,
            )
            for l in range(6):
                j, half = l // 2, l % 2
                where = part * 6 + l
                seen = got_ref[h, part, 144 + l : 145 + l].astype(jnp.int32) - 2 * CAMERAS_PER_BLK * slab
                view[where] = jnp.broadcast_to(jnp.where(seen < 0, seen + cameras, seen), (8, LANES))
                tile = blocks[l][16:24]
                first = [tile[2 + k : 3 + k] for k in range(3)]
                second = [tile[5 + k : 6 + k] for k in range(3)]
                one = rep[0:72, l * LANES : (l + 1) * LANES]
                two = rep[72:144, l * LANES : (l + 1) * LANES]
                for k in range(3):
                    coup[where, k] = one * first[k] + two * second[k]
                at = 6 * half
                for k, m in ((0, 0), (0, 1), (0, 2), (1, 1), (1, 2), (2, 2)):
                    sums[at] = sums[at] + first[k] * first[m] + second[k] * second[m]
                    at += 1
            return tuple(sums)

        sums = lax.fori_loop(0, 4, per_part, tuple(jnp.zeros((1, LANES), jnp.float32) for _ in range(12)))

        inverse = []
        for half in range(2):
            a, b, c, d, e, f = sums[6 * half : 6 * half + 6]
            damp = got_ref[h, 0, 150 + half : 151 + half]
            a, d, f = a + damp, d + damp, f + damp
            cof = [d * f - e * e, c * e - b * f, b * e - c * d, a * f - c * c, b * c - a * e, a * d - b * b]
            det = a * cof[0] + b * cof[1] + c * cof[2]
            cof = [x / det for x in cof]
            inverse.append([[cof[i] for i in order] for order in ((0, 1, 2), (1, 3, 4), (2, 4, 5))])

        group = group_ref[...]

        def gather(first_camera, half):
            halves = []
            for g in range(2):
                base = first_camera + 8 * g
                total = [None] * 3
                for s in range(SLOTS):
                    where = 2 * s + half
                    target = view[where] - base
                    mask = group == jnp.concatenate([target] * 9, axis=0)
                    for k in range(3):
                        term = jnp.where(mask, coup[where, k], 0.0)
                        total[k] = term if s == 0 else total[k] + term
                halves.append(total)
            return [jnp.concatenate([halves[0][k], halves[1][k]], axis=0) for k in range(3)]

        def store(ref, at, k, half, value):
            high, low = split(value)
            lanes = slice(k * TRACKS + half * LANES, k * TRACKS + (half + 1) * LANES)
            if at is None:
                ref[0, :, lanes] = high
                ref[1, :, lanes] = low
            else:
                ref[0, at, :, lanes] = high
                ref[1, at, :, lanes] = low

        for half in range(2):
            panel = gather(CAMERAS_PER_BLK * (2 * h + left_parity), half)
            inv = inverse[half]
            for k in range(3):
                solved = panel[0] * inv[0][k] + panel[1] * inv[1][k] + panel[2] * inv[2][k]
                store(left, None, k, half, solved)

        def per_block(m, _):
            for half in range(2):
                panel = gather(CAMERAS_PER_BLK * (2 * m + right_parity), half)
                for k in range(3):
                    store(right, m, k, half, panel[k])
            return 0

        lax.fori_loop(0, OWNERS, per_block, 0)

        def per_tile(m, _):
            def product(i, j):
                return lax.dot_general(
                    left[i], right[j, m], (((1,), (1,)), ((), ())), preferred_element_type=jnp.float32
                )

            tile = product(0, 0) + (product(0, 1) + product(1, 0))
            at = pl.multiple_of((HOPS - h + m) * TS, 8)
            acc_a[pl.ds(at, TS), :] += tile[:, :LANES]
            acc_b[pl.ds(at, TS), 0 : TS - LANES] += tile[:, LANES:]
            return 0

        lax.fori_loop(0, OWNERS, per_tile, 0)
        return 0

    lax.fori_loop(0, OWNERS, per_slab, 0)

    lane = lax.broadcasted_iota(jnp.int32, (TILES, LANES), 1)

    def flatten(q, _):
        main, tail = [], []
        for i in range(8):
            rows = pl.ds(q * 8 + i, TILES, stride=TS)
            a, b = acc_a[rows, :], acc_b[rows, :]
            main.append(a if i == 0 else pltpu.roll(a, 16 * i, 1))
            tail.append(b if i == 0 else pltpu.roll(b, 16 * i, 1))
        for t in range(9):
            if t == 0:
                value = main[0]
            else:
                value = jnp.where(lane >= 16 * (t - 1), tail[t - 1], main[t - 1])
                if t < 8:
                    value = jnp.where(lane >= 16 * t, main[t], value)
            out_ref[0, 0, :, pl.ds(pl.multiple_of(q * 9 * LANES, LANES) + t * LANES, LANES)] = value
        return 0

    lax.fori_loop(0, TS // 8, flatten, 0)


def tiles(n, got):
    rows = np.arange(TS)
    repeat = np.zeros((TS, 24), np.float32)
    repeat[rows, np.where(rows < 72, rows % 9, 9 + rows % 9)] = 1.0
    repeat = jnp.asarray(np.concatenate([repeat, repeat], axis=1), jnp.bfloat16)
    group = jnp.asarray(np.broadcast_to((np.arange(72) // 9)[:, None], (72, LANES)).astype(np.int32))
    vmem = pl.BlockSpec(memory_space=pltpu.VMEM)
    return pl.pallas_call(
        functools.partial(tiles_body, n),
        out_shape=jax.ShapeDtypeStruct((1, 1, TILES, TS * TS), jnp.float32),
        in_specs=[vmem] * 3,
        out_specs=vmem,
        scratch_shapes=[
            pltpu.VMEM((TS, KC * TRACKS), jnp.float32),
            pltpu.VMEM((2 * SLOTS, 3, 72, LANES), jnp.float32),
            pltpu.VMEM((2 * SLOTS, 8, LANES), jnp.int32),
            pltpu.VMEM((2, TS, 3 * TRACKS), jnp.bfloat16),
            pltpu.VMEM((2, OWNERS, TS, 3 * TRACKS), jnp.bfloat16),
            pltpu.VMEM((TILES * TS, LANES), jnp.float32),
            pltpu.VMEM((TILES * TS, LANES), jnp.float32),
        ],
        compiler_params=pltpu.CompilerParams(vmem_limit_bytes=48 * 2**20),
        name="tiles",
    )(got, repeat, group)


def body(n, residuals, camera_jac, point_jac, obs_index, damping):
    direct = n <= DIRECT_DEVICES
    if direct:
        got = exchange(n, True, damping, residuals, camera_jac, point_jac, obs_index)
    else:
        rows = jnp.concatenate(scaled_rows(residuals, camera_jac, point_jac, obs_index), axis=0)
        rows = lax.all_to_all(rows, "trk", split_axis=1, concat_axis=1, tiled=True)
        got = exchange(n, False, damping, jnp.pad(rows, ((0, 6), (0, 0))))
    return tiles(n, got)


def solution(mesh):
    by_row = P(None, ("trk", "cam"))
    return jax.shard_map(
        functools.partial(body, mesh.shape["trk"]),
        mesh=mesh,
        in_specs=(by_row, by_row, by_row, by_row, P("trk")),
        out_specs=P("trk", "cam", None, None),
        check_vma=False,
    )
```

```python
import functools

import jax
import jax.numpy as jnp
from jax import lax
from jax.experimental import pallas as pl
from jax.experimental.pallas import tpu as pltpu
from jax.sharding import PartitionSpec as P

CAMERAS_PER_BLK = 16
TS = 144
HOPS = 3
OWNERS = HOPS + 1
TILES = 2 * HOPS + 1
KC = 3
TRACKS = 256
SLOTS = 12
LANES = 128
MSG = 152
DIRECT_DEVICES = 8
MESH = pl.DeviceIdType.MESH


def split(x):
    high = x.astype(jnp.bfloat16)
    low = (x - high.astype(jnp.float32)).astype(jnp.bfloat16)
    return high, low


def scaled_rows(residuals, camera_jac, point_jac, index):
    first, second = residuals[0:1], residuals[1:2]
    magnitude = jnp.sqrt(first * first + second * second)
    weight = index[2:3].astype(jnp.float32) / jnp.maximum(magnitude, 1.0)
    root = jnp.sqrt(weight)
    return (
        camera_jac * root,
        point_jac * root,
        index[1:2].astype(jnp.float32),
        index[0:1].astype(jnp.float32),
    )


def fused_body(direct, n, *refs):
    if direct:
        res_hbm, cam_hbm, pnt_hbm, idx_hbm, damp_hbm, out_ref = refs[:6]
        res_ref, cam_ref, pnt_ref, idx_ref, damp_ref = refs[6:11]
        rows_ref, send_ref, recv_ref, ssem1, rsem1 = refs[11:16]
        inputs = (
            (res_hbm, res_ref),
            (cam_hbm, cam_ref),
            (pnt_hbm, pnt_ref),
            (idx_hbm, idx_ref),
            (damp_hbm, damp_ref),
        )
        rest = refs[16:]
    else:
        rows_hbm, damp_hbm, out_ref, rows_ref, damp_ref = refs[:5]
        inputs = ((rows_hbm, rows_ref), (damp_hbm, damp_ref))
        rest = refs[5:]
    insem, ssem2, rsem2, ssem3, rsem3, got_ref, rep, coup, view, left, right, acc_a, acc_b = rest
    me = lax.axis_index("trk")
    col = lax.axis_index("cam")
    core = col + 1 - 2 * lax.rem(col, 2)
    side = lax.rem(col + 2, 4)

    def ahead(by):
        return lax.rem(me + by, n)

    loads = []
    for k, (src, dst) in enumerate(inputs):
        load = pltpu.make_async_copy(src, dst, insem.at[k])
        load.start()
        loads.append(load)
    barrier = pltpu.get_barrier_semaphore()
    steps = range(1, n) if direct else (1, 2, 3, n - 3, n - 2, n - 1)
    for by in steps:
        pl.semaphore_signal(barrier, inc=1, device_id=(ahead(by), col), device_id_type=MESH)
    for other in (core, side):
        pl.semaphore_signal(barrier, inc=1, device_id=(me, other), device_id_type=MESH)
    for load in loads:
        load.wait()

    if direct:
        width = rows_ref.shape[1] // n
        cj, pj, camera, position = scaled_rows(res_ref[...], cam_ref[...], pnt_ref[...], idx_ref[...])
        rows_ref[0:18] = cj
        rows_ref[18:24] = pj
        rows_ref[24:25] = camera
        rows_ref[25:26] = position
        rows_ref[26:32] = jnp.zeros((6, rows_ref.shape[1]), jnp.float32)
        rows = rows_ref[...]
        lane = lax.broadcasted_iota(jnp.int32, (32, LANES), 1)
        row = lax.broadcasted_iota(jnp.int32, (32, LANES), 0)
        fill = jnp.where(row == 25, -1.0, 0.0)
        for e in range(n):
            start = e * width
            piece = rows if start == 0 else pltpu.roll(rows, rows.shape[1] - start, 1)
            send_ref[e] = jnp.where(lane < width, piece[:, :LANES], fill)
    pl.semaphore_wait(barrier, len(steps) + 2)

    copies = []
    if direct:
        for by in range(1, n):
            copy = pltpu.make_async_remote_copy(
                src_ref=send_ref.at[ahead(by)],
                dst_ref=recv_ref.at[by],
                send_sem=ssem1.at[by],
                recv_sem=rsem1.at[by],
                device_id=(ahead(by), col),
                device_id_type=MESH,
            )
            copy.start()
            copies.append(copy)
        recv_ref[0] = send_ref[me]

    acc_a[...] = jnp.zeros_like(acc_a)
    acc_b[...] = jnp.zeros_like(acc_b)
    slot_row = lax.broadcasted_iota(jnp.int32, (72, LANES), 0)
    group = lax.shift_right_logical(slot_row * 57, 9)
    rep_row = lax.broadcasted_iota(jnp.int32, (TS, 48), 0)
    rep_col = lax.broadcasted_iota(jnp.int32, (TS, 48), 1)
    rep_col = jnp.where(rep_col < 24, rep_col, rep_col - 24)
    rep_row = jnp.where(rep_row < 72, rep_row, rep_row - 72)
    second_half = lax.broadcasted_iota(jnp.int32, (TS, 48), 0) >= 72
    parameter = rep_row - 9 * lax.shift_right_logical(rep_row * 57, 9)
    repeat = jnp.where(
        rep_col == jnp.where(second_half, parameter + 9, parameter), 1.0, 0.0
    ).astype(jnp.bfloat16)

    if direct:
        for copy in copies:
            copy.wait_recv()
        chunks = [recv_ref[k] for k in range(n)]
    else:
        chunks = [rows_ref[:, k * LANES : (k + 1) * LANES] for k in range(rows_ref.shape[1] // LANES)]
    slot = lax.broadcasted_iota(jnp.int32, (KC * TRACKS, LANES), 0).astype(jnp.float32)
    places, values = [], []
    for chunk in chunks:
        places.append(jnp.where(slot == chunk[25:26], 1.0, 0.0).astype(jnp.bfloat16))
        high, low = split(chunk)
        values.append(jnp.concatenate([high, low], axis=0))
    placed = lax.dot_general(
        jnp.concatenate(values, axis=1),
        jnp.concatenate(places, axis=1),
        (((1,), (1,)), ((), ())),
        preferred_element_type=jnp.float32,
    )
    placed = placed[:32] + placed[32:]
    tiles = KC * TRACKS // LANES
    for r in range(3):
        for l in range(tiles):
            at = (r * tiles + l) * 8
            got_ref[0, 0, at : at + 8] = placed[8 * r : 8 * r + 8, l * LANES : (l + 1) * LANES]
    for l in range(tiles):
        got_ref[0, 0, 144 + l : 145 + l] = placed[24:25, l * LANES : (l + 1) * LANES]
    for l in range(2):
        got_ref[0, 0, 150 + l : 151 + l] = damp_ref[:, l * LANES : (l + 1) * LANES]

    def message(src, dst, ssem, rsem, device):
        return pltpu.make_async_remote_copy(
            src_ref=src, dst_ref=dst, send_sem=ssem, recv_sem=rsem, device_id=device, device_id_type=MESH
        )

    def along(h):
        return message(got_ref.at[0, 0], got_ref.at[h, 0], ssem2.at[h], rsem2.at[h], (ahead(h), col))

    def to_core(h):
        return message(got_ref.at[h, 0], got_ref.at[h, 1], ssem3.at[h, 1], rsem3.at[h, 1], (me, core))

    def to_side(h):
        return message(got_ref.at[h, 0], got_ref.at[h, 2], ssem3.at[h, 2], rsem3.at[h, 2], (me, side))

    def passed(h):
        return message(got_ref.at[h, 2], got_ref.at[h, 3], ssem3.at[h, 3], rsem3.at[h, 3], (me, core))

    to_side(0).start()
    to_core(0).start()
    for h in range(1, OWNERS):
        along(h).start()
    to_side(0).wait_recv()
    passed(0).start()

    cameras = 2 * n * CAMERAS_PER_BLK
    left_parity = col // 2
    right_parity = lax.rem(col, 2)

    def per_slab(h, _):
        slab = lax.rem(me + n - h, n)
        to_core(h).wait_recv()
        passed(h).wait_recv()

        def per_part(part, sums):
            sums = list(sums)
            blocks = [
                jnp.concatenate(
                    [got_ref[h, part, (r * 6 + l) * 8 : (r * 6 + l) * 8 + 8] for r in range(3)], axis=0
                )
                for l in range(6)
            ]
            high, low = split(jnp.concatenate(blocks, axis=1))
            rep[...] = lax.dot_general(
                repeat,
                jnp.concatenate([high, low], axis=0),
                (((1,), (0,)), ((), ())),
                preferred_element_type=jnp.float32,
            )
            for l in range(6):
                half = l % 2
                where = part * 6 + l
                seen = got_ref[h, part, 144 + l : 145 + l].astype(jnp.int32) - 2 * CAMERAS_PER_BLK * slab
                view[where] = jnp.broadcast_to(jnp.where(seen < 0, seen + cameras, seen), (8, LANES))
                tile = blocks[l][16:24]
                first = [tile[2 + k : 3 + k] for k in range(3)]
                second = [tile[5 + k : 6 + k] for k in range(3)]
                one = rep[0:72, l * LANES : (l + 1) * LANES]
                two = rep[72:144, l * LANES : (l + 1) * LANES]
                for k in range(3):
                    coup[where, k] = one * first[k] + two * second[k]
                at = 6 * half
                for k, m in ((0, 0), (0, 1), (0, 2), (1, 1), (1, 2), (2, 2)):
                    sums[at] = sums[at] + first[k] * first[m] + second[k] * second[m]
                    at += 1
            return tuple(sums)

        sums = lax.fori_loop(0, 4, per_part, tuple(jnp.zeros((1, LANES), jnp.float32) for _ in range(12)))

        @pl.when(h < HOPS)
        def _():
            along(h + 1).wait_recv()
            to_side(h + 1).start()
            to_core(h + 1).start()

        inverse = []
        for half in range(2):
            a, b, c, d, e, f = sums[6 * half : 6 * half + 6]
            damp = got_ref[h, 0, 150 + half : 151 + half]
            a, d, f = a + damp, d + damp, f + damp
            cof = [d * f - e * e, c * e - b * f, b * e - c * d, a * f - c * c, b * c - a * e, a * d - b * b]
            det = a * cof[0] + b * cof[1] + c * cof[2]
            cof = [x / det for x in cof]
            inverse.append([[cof[i] for i in order] for order in ((0, 1, 2), (1, 3, 4), (2, 4, 5))])

        def gather(first_camera, half):
            halves = []
            for g in range(2):
                base = first_camera + 8 * g
                total = [None] * 3
                for s in range(SLOTS):
                    where = 2 * s + half
                    target = view[where] - base
                    mask = group == jnp.concatenate([target] * 9, axis=0)
                    for k in range(3):
                        term = jnp.where(mask, coup[where, k], 0.0)
                        total[k] = term if s == 0 else total[k] + term
                halves.append(total)
            return [jnp.concatenate([halves[0][k], halves[1][k]], axis=0) for k in range(3)]

        def store(ref, k, half, value):
            high, low = split(value)
            lanes = slice(k * TRACKS + half * LANES, k * TRACKS + (half + 1) * LANES)
            ref[0, :, lanes] = high
            ref[1, :, lanes] = low

        for half in range(2):
            panel = gather(CAMERAS_PER_BLK * (2 * h + left_parity), half)
            inv = inverse[half]
            for k in range(3):
                solved = panel[0] * inv[0][k] + panel[1] * inv[1][k] + panel[2] * inv[2][k]
                store(left, k, half, solved)

        for m in range(OWNERS):
            if m == 2:

                @pl.when(h < HOPS)
                def _():
                    to_side(h + 1).wait_recv()
                    passed(h + 1).start()

            for half in range(2):
                panel = gather(CAMERAS_PER_BLK * (2 * m + right_parity), half)
                for k in range(3):
                    store(right.at[m], k, half, panel[k])
            tile = lax.dot_general(
                jnp.concatenate([left[0], left[0], left[1]], axis=1),
                jnp.concatenate([right[m, 0], right[m, 1], right[m, 0]], axis=1),
                (((1,), (1,)), ((), ())),
                preferred_element_type=jnp.float32,
            )
            at = pl.multiple_of((HOPS - h + m) * TS, 8)
            acc_a[pl.ds(at, TS), :] += tile[:, :LANES]
            acc_b[pl.ds(at, TS), 0 : TS - LANES] += tile[:, LANES:]
        return 0

    lax.fori_loop(0, OWNERS, per_slab, 0)

    count = TILES * TS // 8
    lane = lax.broadcasted_iota(jnp.int32, (count, LANES), 1)
    main, tail = None, None
    for t in range(9):
        last_main, last_tail = main, tail
        if t < 8:
            rows = pl.ds(t, count, stride=8)
            main, tail = acc_a[rows, :], acc_b[rows, :]
            if t:
                main, tail = pltpu.roll(main, 16 * t, 1), pltpu.roll(tail, 16 * t, 1)
        if t == 0:
            value = main
        else:
            value = jnp.where(lane >= 16 * (t - 1), last_tail, last_main)
            if t < 8:
                value = jnp.where(lane >= 16 * t, main, value)
        out_ref[pl.ds(t, count, stride=9), :] = value

    for copy in copies:
        copy.wait_send()
    for h in range(OWNERS):
        if h:
            along(h).wait_send()
        to_core(h).wait_send()
        to_side(h).wait_send()
        passed(h).wait_send()


def fused(n, direct, damping, *arrays):
    arrays = arrays + (damping.reshape(1, TRACKS),)
    dma = pltpu.SemaphoreType.DMA
    f32 = jnp.float32
    scratch = [pltpu.VMEM(x.shape, x.dtype) for x in arrays]
    if direct:
        scratch += [
            pltpu.VMEM((32, arrays[0].shape[1]), f32),
            pltpu.VMEM((n, 32, LANES), f32),
            pltpu.VMEM((n, 32, LANES), f32),
            dma((n,)),
            dma((n,)),
        ]
    scratch += [dma((5,)), dma((OWNERS,)), dma((OWNERS,)), dma((OWNERS, 4)), dma((OWNERS, 4))]
    scratch += [
        pltpu.VMEM((OWNERS, 4, MSG, LANES), f32),
        pltpu.VMEM((TS, KC * TRACKS), f32),
        pltpu.VMEM((2 * SLOTS, 3, 72, LANES), f32),
        pltpu.VMEM((2 * SLOTS, 8, LANES), jnp.int32),
        pltpu.VMEM((2, TS, 3 * TRACKS), jnp.bfloat16),
        pltpu.VMEM((OWNERS, 2, TS, 3 * TRACKS), jnp.bfloat16),
        pltpu.VMEM((TILES * TS, LANES), f32),
        pltpu.VMEM((TILES * TS, LANES), f32),
    ]
    out = pl.pallas_call(
        functools.partial(fused_body, direct, n),
        out_shape=jax.ShapeDtypeStruct((TILES * TS * TS // LANES, LANES), f32),
        in_specs=[pl.BlockSpec(memory_space=pltpu.HBM)] * len(arrays),
        out_specs=pl.BlockSpec(memory_space=pltpu.VMEM),
        scratch_shapes=scratch,
        compiler_params=pltpu.CompilerParams(
            collective_id=0, has_side_effects=True, vmem_limit_bytes=64 * 2**20 - 2**15
        ),
        name="fused",
    )(*arrays)
    return out.reshape(1, 1, TILES, TS * TS)


def body(n, residuals, camera_jac, point_jac, obs_index, damping):
    if n <= DIRECT_DEVICES:
        return fused(n, True, damping, residuals, camera_jac, point_jac, obs_index)
    rows = jnp.concatenate(scaled_rows(residuals, camera_jac, point_jac, obs_index), axis=0)
    rows = lax.all_to_all(rows, "trk", split_axis=1, concat_axis=1, tiled=True)
    return fused(n, False, damping, jnp.pad(rows, ((0, 6), (0, 0))))


def solution(mesh):
    by_row = P(None, ("trk", "cam"))
    return jax.shard_map(
        functools.partial(body, mesh.shape["trk"]),
        mesh=mesh,
        in_specs=(by_row, by_row, by_row, by_row, P("trk")),
        out_specs=P("trk", "cam", None, None),
        check_vma=False,
    )
```

```python
import functools

import jax
import jax.numpy as jnp
from jax import lax
from jax.experimental import pallas as pl
from jax.experimental.pallas import tpu as pltpu
from jax.sharding import PartitionSpec as P

CAMERAS_PER_BLK = 16
TS = 144
HOPS = 3
OWNERS = HOPS + 1
TILES = 2 * HOPS + 1
KC = 3
TRACKS = 256
SLOTS = 12
LANES = 128
MSG = 152
DIRECT_DEVICES = 8
MESH = pl.DeviceIdType.MESH


def split(x):
    high = x.astype(jnp.bfloat16)
    low = (x - high.astype(jnp.float32)).astype(jnp.bfloat16)
    return high, low


def scaled_rows(residuals, camera_jac, point_jac, index):
    first, second = residuals[0:1], residuals[1:2]
    magnitude = jnp.sqrt(first * first + second * second)
    weight = index[2:3].astype(jnp.float32) / jnp.maximum(magnitude, 1.0)
    root = jnp.sqrt(weight)
    return (
        camera_jac * root,
        point_jac * root,
        index[1:2].astype(jnp.float32),
        index[0:1].astype(jnp.float32),
    )


def fused_body(direct, n, *refs):
    if direct:
        res_hbm, cam_hbm, pnt_hbm, idx_hbm, damp_hbm, out_ref = refs[:6]
        res_ref, cam_ref, pnt_ref, idx_ref, damp_ref = refs[6:11]
        rows_ref, send_ref, recv_ref, ssem1, rsem1 = refs[11:16]
        inputs = (
            (res_hbm, res_ref),
            (cam_hbm, cam_ref),
            (pnt_hbm, pnt_ref),
            (idx_hbm, idx_ref),
            (damp_hbm, damp_ref),
        )
        rest = refs[16:]
    else:
        rows_hbm, damp_hbm, out_ref, rows_ref, damp_ref = refs[:5]
        inputs = ((rows_hbm, rows_ref), (damp_hbm, damp_ref))
        rest = refs[5:]
    insem, ssem2, rsem2, ssem3, rsem3, got_ref, rep, coup, view, left, right, acc_a, acc_b = rest
    me = lax.axis_index("trk")
    col = lax.axis_index("cam")
    core = col + 1 - 2 * lax.rem(col, 2)
    side = lax.rem(col + 2, 4)

    def ahead(by):
        return lax.rem(me + by, n)

    loads = []
    for k, (src, dst) in enumerate(inputs):
        load = pltpu.make_async_copy(src, dst, insem.at[k])
        load.start()
        loads.append(load)
    barrier = pltpu.get_barrier_semaphore()
    steps = range(1, n) if direct else (1, 2, 3, n - 3, n - 2, n - 1)
    for by in steps:
        pl.semaphore_signal(barrier, inc=1, device_id=(ahead(by), col), device_id_type=MESH)
    for other in (core, side):
        pl.semaphore_signal(barrier, inc=1, device_id=(me, other), device_id_type=MESH)
    for load in loads:
        load.wait()

    if direct:
        width = rows_ref.shape[1] // n
        cj, pj, camera, position = scaled_rows(res_ref[...], cam_ref[...], pnt_ref[...], idx_ref[...])
        rows_ref[0:18] = cj
        rows_ref[18:24] = pj
        rows_ref[24:25] = camera
        rows_ref[25:26] = position
        rows_ref[26:32] = jnp.zeros((6, rows_ref.shape[1]), jnp.float32)
        rows = rows_ref[...]
        lane = lax.broadcasted_iota(jnp.int32, (32, LANES), 1)
        row = lax.broadcasted_iota(jnp.int32, (32, LANES), 0)
        fill = jnp.where(row == 25, -1.0, 0.0)
        for e in range(n):
            start = e * width
            piece = rows if start == 0 else pltpu.roll(rows, rows.shape[1] - start, 1)
            send_ref[e] = jnp.where(lane < width, piece[:, :LANES], fill)
    pl.semaphore_wait(barrier, len(steps) + 2)

    copies = []
    if direct:
        for by in range(1, n):
            copy = pltpu.make_async_remote_copy(
                src_ref=send_ref.at[ahead(by)],
                dst_ref=recv_ref.at[by],
                send_sem=ssem1.at[by],
                recv_sem=rsem1.at[by],
                device_id=(ahead(by), col),
                device_id_type=MESH,
            )
            copy.start()
            copies.append(copy)
        recv_ref[0] = send_ref[me]

    acc_a[...] = jnp.zeros_like(acc_a)
    acc_b[...] = jnp.zeros_like(acc_b)
    slot_row = lax.broadcasted_iota(jnp.int32, (72, LANES), 0)
    group = lax.shift_right_logical(slot_row * 57, 9)
    rep_row = lax.broadcasted_iota(jnp.int32, (TS, 48), 0)
    rep_col = lax.broadcasted_iota(jnp.int32, (TS, 48), 1)
    rep_col = jnp.where(rep_col < 24, rep_col, rep_col - 24)
    rep_row = jnp.where(rep_row < 72, rep_row, rep_row - 72)
    second_half = lax.broadcasted_iota(jnp.int32, (TS, 48), 0) >= 72
    parameter = rep_row - 9 * lax.shift_right_logical(rep_row * 57, 9)
    repeat = jnp.where(
        rep_col == jnp.where(second_half, parameter + 9, parameter), 1.0, 0.0
    ).astype(jnp.bfloat16)

    if direct:
        for copy in copies:
            copy.wait_recv()
        chunks = [recv_ref[k] for k in range(n)]
    else:
        chunks = [rows_ref[:, k * LANES : (k + 1) * LANES] for k in range(rows_ref.shape[1] // LANES)]
    slot = lax.broadcasted_iota(jnp.int32, (KC * TRACKS, LANES), 0).astype(jnp.float32)
    places, values = [], []
    for chunk in chunks:
        places.append(jnp.where(slot == chunk[25:26], 1.0, 0.0).astype(jnp.bfloat16))
        high, low = split(chunk)
        values.append(jnp.concatenate([high, low], axis=0))
    placed = lax.dot_general(
        jnp.concatenate(values, axis=1),
        jnp.concatenate(places, axis=1),
        (((1,), (1,)), ((), ())),
        preferred_element_type=jnp.float32,
    )
    placed = placed[:32] + placed[32:]
    tiles = KC * TRACKS // LANES
    for r in range(3):
        for l in range(tiles):
            at = (r * tiles + l) * 8
            got_ref[0, 0, at : at + 8] = placed[8 * r : 8 * r + 8, l * LANES : (l + 1) * LANES]
    for l in range(tiles):
        got_ref[0, 0, 144 + l : 145 + l] = placed[24:25, l * LANES : (l + 1) * LANES]
    for l in range(2):
        got_ref[0, 0, 150 + l : 151 + l] = damp_ref[:, l * LANES : (l + 1) * LANES]

    def message(src, dst, ssem, rsem, device):
        return pltpu.make_async_remote_copy(
            src_ref=src, dst_ref=dst, send_sem=ssem, recv_sem=rsem, device_id=device, device_id_type=MESH
        )

    def along(h):
        return message(got_ref.at[0, 0], got_ref.at[h, 0], ssem2.at[h], rsem2.at[h], (ahead(h), col))

    def to_core(h):
        return message(got_ref.at[h, 0], got_ref.at[h, 1], ssem3.at[h, 1], rsem3.at[h, 1], (me, core))

    def to_side(h):
        return message(got_ref.at[h, 0], got_ref.at[h, 2], ssem3.at[h, 2], rsem3.at[h, 2], (me, side))

    def passed(h):
        return message(got_ref.at[h, 2], got_ref.at[h, 3], ssem3.at[h, 3], rsem3.at[h, 3], (me, core))

    to_side(0).start()
    to_core(0).start()
    for h in range(1, OWNERS):
        along(h).start()
    to_side(0).wait_recv()
    passed(0).start()
    along(1).wait_recv()
    to_side(1).start()
    to_core(1).start()

    cameras = 2 * n * CAMERAS_PER_BLK
    left_parity = col // 2
    right_parity = lax.rem(col, 2)

    def per_slab(h, _):
        slab = lax.rem(me + n - h, n)
        to_core(h).wait_recv()
        passed(h).wait_recv()

        def per_part(part, sums):
            sums = list(sums)
            blocks = [
                jnp.concatenate(
                    [got_ref[h, part, (r * 6 + l) * 8 : (r * 6 + l) * 8 + 8] for r in range(3)], axis=0
                )
                for l in range(6)
            ]
            high, low = split(jnp.concatenate(blocks, axis=1))
            rep[...] = lax.dot_general(
                repeat,
                jnp.concatenate([high, low], axis=0),
                (((1,), (0,)), ((), ())),
                preferred_element_type=jnp.float32,
            )
            for l in range(6):
                half = l % 2
                where = part * 6 + l
                seen = got_ref[h, part, 144 + l : 145 + l].astype(jnp.int32) - 2 * CAMERAS_PER_BLK * slab
                view[where] = jnp.broadcast_to(jnp.where(seen < 0, seen + cameras, seen), (8, LANES))
                tile = blocks[l][16:24]
                first = [tile[2 + k : 3 + k] for k in range(3)]
                second = [tile[5 + k : 6 + k] for k in range(3)]
                one = rep[0:72, l * LANES : (l + 1) * LANES]
                two = rep[72:144, l * LANES : (l + 1) * LANES]
                for k in range(3):
                    coup[where, k] = one * first[k] + two * second[k]
                at = 6 * half
                for k, m in ((0, 0), (0, 1), (0, 2), (1, 1), (1, 2), (2, 2)):
                    sums[at] = sums[at] + first[k] * first[m] + second[k] * second[m]
                    at += 1
            return tuple(sums)

        sums = lax.fori_loop(0, 4, per_part, tuple(jnp.zeros((1, LANES), jnp.float32) for _ in range(12)))

        @pl.when(h < HOPS - 1)
        def _():
            along(h + 2).wait_recv()
            to_side(h + 2).start()
            to_core(h + 2).start()

        inverse = []
        for half in range(2):
            a, b, c, d, e, f = sums[6 * half : 6 * half + 6]
            damp = got_ref[h, 0, 150 + half : 151 + half]
            a, d, f = a + damp, d + damp, f + damp
            cof = [d * f - e * e, c * e - b * f, b * e - c * d, a * f - c * c, b * c - a * e, a * d - b * b]
            det = a * cof[0] + b * cof[1] + c * cof[2]
            cof = [x / det for x in cof]
            inverse.append([[cof[i] for i in order] for order in ((0, 1, 2), (1, 3, 4), (2, 4, 5))])

        def gather(first_camera, half):
            halves = []
            for g in range(2):
                base = first_camera + 8 * g
                total = [None] * 3
                for s in range(SLOTS):
                    where = 2 * s + half
                    target = view[where] - base
                    mask = group == jnp.concatenate([target] * 9, axis=0)
                    for k in range(3):
                        term = jnp.where(mask, coup[where, k], 0.0)
                        total[k] = term if s == 0 else total[k] + term
                halves.append(total)
            return [jnp.concatenate([halves[0][k], halves[1][k]], axis=0) for k in range(3)]

        def store(ref, k, half, value):
            high, low = split(value)
            lanes = slice(k * TRACKS + half * LANES, k * TRACKS + (half + 1) * LANES)
            ref[0, :, lanes] = high
            ref[1, :, lanes] = low

        for half in range(2):
            panel = gather(CAMERAS_PER_BLK * (2 * h + left_parity), half)
            inv = inverse[half]
            for k in range(3):
                solved = panel[0] * inv[0][k] + panel[1] * inv[1][k] + panel[2] * inv[2][k]
                store(left, k, half, solved)

        for m in range(OWNERS):
            if m == 2:

                @pl.when(h < HOPS)
                def _():
                    to_side(h + 1).wait_recv()
                    passed(h + 1).start()

            for half in range(2):
                panel = gather(CAMERAS_PER_BLK * (2 * m + right_parity), half)
                for k in range(3):
                    store(right.at[m], k, half, panel[k])
            tile = lax.dot_general(
                jnp.concatenate([left[0], left[0], left[1]], axis=1),
                jnp.concatenate([right[m, 0], right[m, 1], right[m, 0]], axis=1),
                (((1,), (1,)), ((), ())),
                preferred_element_type=jnp.float32,
            )
            at = pl.multiple_of((HOPS - h + m) * TS, 8)
            acc_a[pl.ds(at, TS), :] += tile[:, :LANES]
            acc_b[pl.ds(at, TS), 0 : TS - LANES] += tile[:, LANES:]
        return 0

    lax.fori_loop(0, OWNERS, per_slab, 0)

    count = TILES * TS // 8
    lane = lax.broadcasted_iota(jnp.int32, (count, LANES), 1)
    main, tail = None, None
    for t in range(9):
        last_main, last_tail = main, tail
        if t < 8:
            rows = pl.ds(t, count, stride=8)
            main, tail = acc_a[rows, :], acc_b[rows, :]
            if t:
                main, tail = pltpu.roll(main, 16 * t, 1), pltpu.roll(tail, 16 * t, 1)
        if t == 0:
            value = main
        else:
            value = jnp.where(lane >= 16 * (t - 1), last_tail, last_main)
            if t < 8:
                value = jnp.where(lane >= 16 * t, main, value)
        out_ref[pl.ds(t, count, stride=9), :] = value

    for copy in copies:
        copy.wait_send()
    for h in range(OWNERS):
        if h:
            along(h).wait_send()
        to_core(h).wait_send()
        to_side(h).wait_send()
        passed(h).wait_send()


def fused(n, direct, damping, *arrays):
    arrays = arrays + (damping.reshape(1, TRACKS),)
    dma = pltpu.SemaphoreType.DMA
    f32 = jnp.float32
    scratch = [pltpu.VMEM(x.shape, x.dtype) for x in arrays]
    if direct:
        scratch += [
            pltpu.VMEM((32, arrays[0].shape[1]), f32),
            pltpu.VMEM((n, 32, LANES), f32),
            pltpu.VMEM((n, 32, LANES), f32),
            dma((n,)),
            dma((n,)),
        ]
    scratch += [dma((5,)), dma((OWNERS,)), dma((OWNERS,)), dma((OWNERS, 4)), dma((OWNERS, 4))]
    scratch += [
        pltpu.VMEM((OWNERS, 4, MSG, LANES), f32),
        pltpu.VMEM((TS, KC * TRACKS), f32),
        pltpu.VMEM((2 * SLOTS, 3, 72, LANES), f32),
        pltpu.VMEM((2 * SLOTS, 8, LANES), jnp.int32),
        pltpu.VMEM((2, TS, 3 * TRACKS), jnp.bfloat16),
        pltpu.VMEM((OWNERS, 2, TS, 3 * TRACKS), jnp.bfloat16),
        pltpu.VMEM((TILES * TS, LANES), f32),
        pltpu.VMEM((TILES * TS, LANES), f32),
    ]
    out = pl.pallas_call(
        functools.partial(fused_body, direct, n),
        out_shape=jax.ShapeDtypeStruct((TILES * TS * TS // LANES, LANES), f32),
        in_specs=[pl.BlockSpec(memory_space=pltpu.HBM)] * len(arrays),
        out_specs=pl.BlockSpec(memory_space=pltpu.VMEM),
        scratch_shapes=scratch,
        compiler_params=pltpu.CompilerParams(
            collective_id=0, has_side_effects=True, vmem_limit_bytes=64 * 2**20 - 2**15
        ),
        name="fused",
    )(*arrays)
    return out.reshape(1, 1, TILES, TS * TS)


def body(n, residuals, camera_jac, point_jac, obs_index, damping):
    if n <= DIRECT_DEVICES:
        return fused(n, True, damping, residuals, camera_jac, point_jac, obs_index)
    rows = jnp.concatenate(scaled_rows(residuals, camera_jac, point_jac, obs_index), axis=0)
    rows = lax.all_to_all(rows, "trk", split_axis=1, concat_axis=1, tiled=True)
    return fused(n, False, damping, jnp.pad(rows, ((0, 6), (0, 0))))


def solution(mesh):
    by_row = P(None, ("trk", "cam"))
    return jax.shard_map(
        functools.partial(body, mesh.shape["trk"]),
        mesh=mesh,
        in_specs=(by_row, by_row, by_row, by_row, P("trk")),
        out_specs=P("trk", "cam", None, None),
        check_vma=False,
    )
```

```python
import functools

import jax
import jax.numpy as jnp
from jax import lax
from jax.experimental import pallas as pl
from jax.experimental.pallas import tpu as pltpu
from jax.sharding import PartitionSpec as P

CAMERAS_PER_BLK = 16
TS = 144
HOPS = 3
OWNERS = HOPS + 1
TILES = 2 * HOPS + 1
KC = 3
TRACKS = 256
SLOTS = 12
LANES = 128
MSG = 152
DIRECT_DEVICES = 8
MESH = pl.DeviceIdType.MESH


def split(x):
    high = x.astype(jnp.bfloat16)
    low = (x - high.astype(jnp.float32)).astype(jnp.bfloat16)
    return high, low


def scaled_rows(residuals, camera_jac, point_jac, index):
    first, second = residuals[0:1], residuals[1:2]
    magnitude = jnp.sqrt(first * first + second * second)
    weight = index[2:3].astype(jnp.float32) / jnp.maximum(magnitude, 1.0)
    root = jnp.sqrt(weight)
    return (
        camera_jac * root,
        point_jac * root,
        index[1:2].astype(jnp.float32),
        index[0:1].astype(jnp.float32),
    )


def fused_body(direct, n, *refs):
    if direct:
        res_hbm, cam_hbm, pnt_hbm, idx_hbm, damp_hbm, out_ref = refs[:6]
        res_ref, cam_ref, pnt_ref, idx_ref, damp_ref = refs[6:11]
        rows_ref, send_ref, recv_ref, ssem1, rsem1 = refs[11:16]
        inputs = (
            (res_hbm, res_ref),
            (cam_hbm, cam_ref),
            (pnt_hbm, pnt_ref),
            (idx_hbm, idx_ref),
            (damp_hbm, damp_ref),
        )
        rest = refs[16:]
    else:
        rows_hbm, damp_hbm, out_ref, rows_ref, damp_ref = refs[:5]
        inputs = ((rows_hbm, rows_ref), (damp_hbm, damp_ref))
        rest = refs[5:]
    insem, ssem2, rsem2, ssem3, rsem3, got_ref, rep, coup, view, left, right, acc_a, acc_b = rest
    me = lax.axis_index("trk")
    col = lax.axis_index("cam")
    core = col + 1 - 2 * lax.rem(col, 2)
    side = lax.rem(col + 2, 4)

    def ahead(by):
        return lax.rem(me + by, n)

    loads = []
    for k, (src, dst) in enumerate(inputs):
        load = pltpu.make_async_copy(src, dst, insem.at[k])
        load.start()
        loads.append(load)
    barrier = pltpu.get_barrier_semaphore()
    steps = range(1, n) if direct else (1, 2, 3, n - 3, n - 2, n - 1)
    for by in steps:
        pl.semaphore_signal(barrier, inc=1, device_id=(ahead(by), col), device_id_type=MESH)
    for other in (core, side):
        pl.semaphore_signal(barrier, inc=1, device_id=(me, other), device_id_type=MESH)
    for load in loads:
        load.wait()

    if direct:
        width = rows_ref.shape[1] // n
        cj, pj, camera, position = scaled_rows(res_ref[...], cam_ref[...], pnt_ref[...], idx_ref[...])
        rows_ref[0:18] = cj
        rows_ref[18:24] = pj
        rows_ref[24:25] = camera
        rows_ref[25:26] = position
        rows_ref[26:32] = jnp.zeros((6, rows_ref.shape[1]), jnp.float32)
        rows = rows_ref[...]
        lane = lax.broadcasted_iota(jnp.int32, (32, LANES), 1)
        row = lax.broadcasted_iota(jnp.int32, (32, LANES), 0)
        fill = jnp.where(row == 25, -1.0, 0.0)
        for e in range(n):
            start = e * width
            piece = rows if start == 0 else pltpu.roll(rows, rows.shape[1] - start, 1)
            send_ref[e] = jnp.where(lane < width, piece[:, :LANES], fill)
    pl.semaphore_wait(barrier, len(steps) + 2)

    copies = []
    if direct:
        for by in range(1, n):
            copy = pltpu.make_async_remote_copy(
                src_ref=send_ref.at[ahead(by)],
                dst_ref=recv_ref.at[by],
                send_sem=ssem1.at[by],
                recv_sem=rsem1.at[by],
                device_id=(ahead(by), col),
                device_id_type=MESH,
            )
            copy.start()
            copies.append(copy)
        recv_ref[0] = send_ref[me]

    acc_a[...] = jnp.zeros_like(acc_a)
    acc_b[...] = jnp.zeros_like(acc_b)
    slot_row = lax.broadcasted_iota(jnp.int32, (72, LANES), 0)
    group = lax.shift_right_logical(slot_row * 57, 9)
    rep_row = lax.broadcasted_iota(jnp.int32, (TS, 48), 0)
    rep_col = lax.broadcasted_iota(jnp.int32, (TS, 48), 1)
    rep_col = jnp.where(rep_col < 24, rep_col, rep_col - 24)
    rep_row = jnp.where(rep_row < 72, rep_row, rep_row - 72)
    second_half = lax.broadcasted_iota(jnp.int32, (TS, 48), 0) >= 72
    parameter = rep_row - 9 * lax.shift_right_logical(rep_row * 57, 9)
    repeat = jnp.where(
        rep_col == jnp.where(second_half, parameter + 9, parameter), 1.0, 0.0
    ).astype(jnp.bfloat16)

    if direct:
        for copy in copies:
            copy.wait_recv()
        chunks = [recv_ref[k] for k in range(n)]
    else:
        chunks = [rows_ref[:, k * LANES : (k + 1) * LANES] for k in range(rows_ref.shape[1] // LANES)]
    slot = lax.broadcasted_iota(jnp.int32, (KC * TRACKS, LANES), 0).astype(jnp.float32)
    places, values = [], []
    for chunk in chunks:
        places.append(jnp.where(slot == chunk[25:26], 1.0, 0.0).astype(jnp.bfloat16))
        high, low = split(chunk)
        values.append(jnp.concatenate([high, low], axis=0))
    placed = lax.dot_general(
        jnp.concatenate(values, axis=1),
        jnp.concatenate(places, axis=1),
        (((1,), (1,)), ((), ())),
        preferred_element_type=jnp.float32,
    )
    placed = placed[:32] + placed[32:]
    tiles = KC * TRACKS // LANES
    for r in range(3):
        for l in range(tiles):
            at = (r * tiles + l) * 8
            got_ref[0, 0, at : at + 8] = placed[8 * r : 8 * r + 8, l * LANES : (l + 1) * LANES]
    for l in range(tiles):
        got_ref[0, 0, 144 + l : 145 + l] = placed[24:25, l * LANES : (l + 1) * LANES]
    for l in range(2):
        got_ref[0, 0, 150 + l : 151 + l] = damp_ref[:, l * LANES : (l + 1) * LANES]

    def message(src, dst, ssem, rsem, device):
        return pltpu.make_async_remote_copy(
            src_ref=src, dst_ref=dst, send_sem=ssem, recv_sem=rsem, device_id=device, device_id_type=MESH
        )

    def along(h):
        return message(got_ref.at[0, 0], got_ref.at[h, 0], ssem2.at[h], rsem2.at[h], (ahead(h), col))

    def to_core(h):
        return message(got_ref.at[h, 0], got_ref.at[h, 1], ssem3.at[h, 1], rsem3.at[h, 1], (me, core))

    def to_side(h):
        return message(got_ref.at[h, 0], got_ref.at[h, 2], ssem3.at[h, 2], rsem3.at[h, 2], (me, side))

    def passed(h):
        return message(got_ref.at[h, 2], got_ref.at[h, 3], ssem3.at[h, 3], rsem3.at[h, 3], (me, core))

    to_side(0).start()
    to_core(0).start()
    for h in range(1, OWNERS):
        along(h).start()
    to_side(0).wait_recv()
    passed(0).start()
    along(1).wait_recv()
    to_side(1).start()
    to_core(1).start()

    cameras = 2 * n * CAMERAS_PER_BLK
    left_parity = col // 2
    right_parity = lax.rem(col, 2)

    def per_slab(h, _):
        slab = lax.rem(me + n - h, n)
        to_core(h).wait_recv()
        passed(h).wait_recv()

        def per_part(part, sums):
            sums = list(sums)
            blocks = [
                jnp.concatenate(
                    [got_ref[h, part, (r * 6 + l) * 8 : (r * 6 + l) * 8 + 8] for r in range(3)], axis=0
                )
                for l in range(6)
            ]
            high, low = split(jnp.concatenate(blocks, axis=1))
            rep[...] = lax.dot_general(
                repeat,
                jnp.concatenate([high, low], axis=0),
                (((1,), (0,)), ((), ())),
                preferred_element_type=jnp.float32,
            )
            for l in range(6):
                half = l % 2
                where = part * 6 + l
                seen = got_ref[h, part, 144 + l : 145 + l].astype(jnp.int32) - 2 * CAMERAS_PER_BLK * slab
                view[where] = jnp.broadcast_to(jnp.where(seen < 0, seen + cameras, seen), (8, LANES))
                tile = blocks[l][16:24]
                first = [tile[2 + k : 3 + k] for k in range(3)]
                second = [tile[5 + k : 6 + k] for k in range(3)]
                one = rep[0:72, l * LANES : (l + 1) * LANES]
                two = rep[72:144, l * LANES : (l + 1) * LANES]
                for k in range(3):
                    coup[where, k] = one * first[k] + two * second[k]
                at = 6 * half
                for k, m in ((0, 0), (0, 1), (0, 2), (1, 1), (1, 2), (2, 2)):
                    sums[at] = sums[at] + first[k] * first[m] + second[k] * second[m]
                    at += 1
            return tuple(sums)

        sums = lax.fori_loop(0, 4, per_part, tuple(jnp.zeros((1, LANES), jnp.float32) for _ in range(12)))

        @pl.when(h < HOPS - 1)
        def _():
            along(h + 2).wait_recv()
            to_side(h + 2).start()
            to_core(h + 2).start()

        inverse = []
        for half in range(2):
            a, b, c, d, e, f = sums[6 * half : 6 * half + 6]
            damp = got_ref[h, 0, 150 + half : 151 + half]
            a, d, f = a + damp, d + damp, f + damp
            cof = [d * f - e * e, c * e - b * f, b * e - c * d, a * f - c * c, b * c - a * e, a * d - b * b]
            det = a * cof[0] + b * cof[1] + c * cof[2]
            cof = [x / det for x in cof]
            inverse.append([[cof[i] for i in order] for order in ((0, 1, 2), (1, 3, 4), (2, 4, 5))])

        def gather(first_camera, half):
            halves = []
            for g in range(2):
                base = first_camera + 8 * g
                total = [None] * 3
                for s in range(SLOTS):
                    where = 2 * s + half
                    target = view[where] - base
                    mask = group == jnp.concatenate([target] * 9, axis=0)
                    for k in range(3):
                        term = jnp.where(mask, coup[where, k], 0.0)
                        total[k] = term if s == 0 else total[k] + term
                halves.append(total)
            return [jnp.concatenate([halves[0][k], halves[1][k]], axis=0) for k in range(3)]

        def store(ref, k, half, value):
            high, low = split(value)
            lanes = slice(k * TRACKS + half * LANES, k * TRACKS + (half + 1) * LANES)
            ref[0, :, lanes] = high
            ref[1, :, lanes] = low

        for half in range(2):
            panel = gather(CAMERAS_PER_BLK * (2 * h + left_parity), half)
            inv = inverse[half]
            for k in range(3):
                solved = panel[0] * inv[0][k] + panel[1] * inv[1][k] + panel[2] * inv[2][k]
                store(left, k, half, solved)

        for m in range(OWNERS):
            if m == 1:

                @pl.when(h < HOPS)
                def _():
                    to_side(h + 1).wait_recv()
                    passed(h + 1).start()

            for half in range(2):
                panel = gather(CAMERAS_PER_BLK * (2 * m + right_parity), half)
                for k in range(3):
                    store(right.at[m], k, half, panel[k])
            tile = lax.dot_general(
                jnp.concatenate([left[0], left[0], left[1]], axis=1),
                jnp.concatenate([right[m, 0], right[m, 1], right[m, 0]], axis=1),
                (((1,), (1,)), ((), ())),
                preferred_element_type=jnp.float32,
            )
            at = pl.multiple_of((HOPS - h + m) * TS, 8)
            acc_a[pl.ds(at, TS), :] += tile[:, :LANES]
            acc_b[pl.ds(at, TS), 0 : TS - LANES] += tile[:, LANES:]
        return 0

    lax.fori_loop(0, OWNERS, per_slab, 0)

    count = TILES * TS // 8
    lane = lax.broadcasted_iota(jnp.int32, (count, LANES), 1)
    main, tail = None, None
    for t in range(9):
        last_main, last_tail = main, tail
        if t < 8:
            rows = pl.ds(t, count, stride=8)
            main, tail = acc_a[rows, :], acc_b[rows, :]
            if t:
                main, tail = pltpu.roll(main, 16 * t, 1), pltpu.roll(tail, 16 * t, 1)
        if t == 0:
            value = main
        else:
            value = jnp.where(lane >= 16 * (t - 1), last_tail, last_main)
            if t < 8:
                value = jnp.where(lane >= 16 * t, main, value)
        out_ref[pl.ds(t, count, stride=9), :] = value

    for copy in copies:
        copy.wait_send()
    for h in range(OWNERS):
        if h:
            along(h).wait_send()
        to_core(h).wait_send()
        to_side(h).wait_send()
        passed(h).wait_send()


def fused(n, direct, damping, *arrays):
    arrays = arrays + (damping.reshape(1, TRACKS),)
    dma = pltpu.SemaphoreType.DMA
    f32 = jnp.float32
    scratch = [pltpu.VMEM(x.shape, x.dtype) for x in arrays]
    if direct:
        scratch += [
            pltpu.VMEM((32, arrays[0].shape[1]), f32),
            pltpu.VMEM((n, 32, LANES), f32),
            pltpu.VMEM((n, 32, LANES), f32),
            dma((n,)),
            dma((n,)),
        ]
    scratch += [dma((5,)), dma((OWNERS,)), dma((OWNERS,)), dma((OWNERS, 4)), dma((OWNERS, 4))]
    scratch += [
        pltpu.VMEM((OWNERS, 4, MSG, LANES), f32),
        pltpu.VMEM((TS, KC * TRACKS), f32),
        pltpu.VMEM((2 * SLOTS, 3, 72, LANES), f32),
        pltpu.VMEM((2 * SLOTS, 8, LANES), jnp.int32),
        pltpu.VMEM((2, TS, 3 * TRACKS), jnp.bfloat16),
        pltpu.VMEM((OWNERS, 2, TS, 3 * TRACKS), jnp.bfloat16),
        pltpu.VMEM((TILES * TS, LANES), f32),
        pltpu.VMEM((TILES * TS, LANES), f32),
    ]
    out = pl.pallas_call(
        functools.partial(fused_body, direct, n),
        out_shape=jax.ShapeDtypeStruct((TILES * TS * TS // LANES, LANES), f32),
        in_specs=[pl.BlockSpec(memory_space=pltpu.HBM)] * len(arrays),
        out_specs=pl.BlockSpec(memory_space=pltpu.VMEM),
        scratch_shapes=scratch,
        compiler_params=pltpu.CompilerParams(
            collective_id=0, has_side_effects=True, vmem_limit_bytes=64 * 2**20 - 2**15
        ),
        name="fused",
    )(*arrays)
    return out.reshape(1, 1, TILES, TS * TS)


def body(n, residuals, camera_jac, point_jac, obs_index, damping):
    if n <= DIRECT_DEVICES:
        return fused(n, True, damping, residuals, camera_jac, point_jac, obs_index)
    rows = jnp.concatenate(scaled_rows(residuals, camera_jac, point_jac, obs_index), axis=0)
    rows = lax.all_to_all(rows, "trk", split_axis=1, concat_axis=1, tiled=True)
    return fused(n, False, damping, jnp.pad(rows, ((0, 6), (0, 0))))


def solution(mesh):
    by_row = P(None, ("trk", "cam"))
    return jax.shard_map(
        functools.partial(body, mesh.shape["trk"]),
        mesh=mesh,
        in_specs=(by_row, by_row, by_row, by_row, P("trk")),
        out_specs=P("trk", "cam", None, None),
        check_vma=False,
    )
```
